32 devices in a mesh: pool: 8 (over z, y), head: 4 (over x, core).
Axes of the slice: x: 2, y: 2, z: 4, core: 2. Of those that a mesh axis runs over, the one named last changes fastest.
Arguments:
- queries: bfloat16 [8, 256, 8192], P('pool', None, 'head'), may hold values from -6 to 6
- new_kv: bfloat16 [8, 256, 2048], P('pool', None, 'head'), may hold values from -6 to 6
- pool: bfloat16 [256, 256, 2048], P('pool', None, 'head'), may hold values from -6 to 6
- page_owner: int32 [8, 32], replicated, may hold values from 0 to 7, as said below
- page_slot: int32 [8, 32], replicated, may hold values from 0 to 31, as said below
- cached_len: int32 [8], replicated, may hold values from 1 to 8192, as said below
Outputs:
- attended: bfloat16 [8, 256, 8192], P('pool', None, 'head')
The draws below stay inside these ranges and needn't reach their ends.
Inputs may be any that keep to these rules, and one draw needn't show every extreme that they name: `page_owner`: each of the 32 entries of a row is the owner of that page of the request; every owner holds exactly 4 entries of each row. Pairs (page_owner, page_slot) are distinct over all requests and pages. Request r uses its first ceil(cached_len[r] / 256) pages; some request has exactly 8192 cached tokens.
All inputs are finite; a program needn't handle non-finite values.
Results may differ from the reference program's by a relative error of at most 0.0075.
Values may be sent and summed in bfloat16 or wider, within the bound.
A program may use at most 64 MiB of HBM per device.

```python
import math
import jax
import jax.numpy as jnp
from jax import lax

QH = 64
KVH = 8
HD = 128
PAGE = 256
MAXPG = 32
NEW = 256
REQS = 8
PAGES_DEV = 32
CTX = 8192
N_POOL = 8


def page_tables(key):
    perm_key = jax.random.fold_in(key, 21)
    slot_key = jax.random.fold_in(key, 22)
    owner_perm = jax.vmap(lambda subkey: jax.random.permutation(subkey, N_POOL))(jax.random.split(perm_key, REQS))
    slot_perm = jax.vmap(lambda subkey: jax.random.permutation(subkey, PAGES_DEV))(jax.random.split(slot_key, N_POOL))
    per_owner = MAXPG // N_POOL
    page_numbers = jnp.arange(MAXPG, dtype=jnp.int32)
    owners = owner_perm[:, page_numbers % N_POOL]
    local_rank = jnp.arange(REQS, dtype=jnp.int32)[:, None] * per_owner + (page_numbers // N_POOL)[None, :]
    slots = slot_perm[owners, local_rank]
    return (owners.astype(jnp.int32), slots.astype(jnp.int32))


def draw_page_owner(key, part):
    return page_tables(key)[0]


def draw_page_slot(key, part):
    return page_tables(key)[1]


def draw_cached_len(key, part):
    lengths = jax.random.randint(jax.random.fold_in(key, 31), (REQS,), 1, MAXPG * PAGE + 1)
    longest = jax.random.randint(jax.random.fold_in(key, 32), (), 0, REQS)
    lengths = jnp.where(jnp.arange(REQS) == longest, MAXPG * PAGE, lengths)
    return lengths.astype(jnp.int32)


def draw_queries(key, part):
    sample_key = jax.random.fold_in(key, 11)
    shape = (REQS, NEW, QH * HD)
    sample = jnp.clip(jax.random.normal(sample_key, shape, jnp.float32), -6.0, 6.0)
    return sample.astype(jnp.bfloat16)


def draw_pool(key, part):
    sample_key = jax.random.fold_in(key, 12)
    shape = (N_POOL * PAGES_DEV, PAGE, KVH * 2 * HD)
    sample = jnp.clip(jax.random.normal(sample_key, shape, jnp.float32), -6.0, 6.0)
    return sample.astype(jnp.bfloat16)


def levels(own_key, shape, shards, low, high):
    def one(position, blocks):
        heights = jax.random.uniform(jax.random.fold_in(jax.random.fold_in(own_key, 6), position), (blocks,), jnp.float32, low / len(shards), high / len(shards))
        return jnp.repeat(jnp.exp(heights), shape[position] // blocks).reshape((-1,) + (1,) * (len(shape) - position - 1))

    level = one(*shards[0])
    for cut in shards[1:]:
        level = level * one(*cut)
    return level


def noise(stream_key, extent, width, reach, cuts=(), kind=jnp.bfloat16):
    gain = levels(stream_key, extent, cuts, -0.22, 0.18) if cuts else 1.0
    values = jax.random.normal(stream_key, extent, jnp.float32) * width * gain
    return jnp.minimum(jnp.maximum(values, -reach), reach).astype(kind)


def setup_inputs(seed: int = 0) -> dict:
    streams_of = jax.random.split(jax.random.key(seed), 7)
    return {
        "queries": draw_queries(jax.random.fold_in(streams_of[6], 71), 0),
        "new_kv": noise(streams_of[1], (REQS, NEW, KVH * 2 * HD), 1.0, 6.0, ((0, 8), (2, 4))),
        "pool": draw_pool(jax.random.fold_in(streams_of[6], 71), 0),
        "page_owner": draw_page_owner(jax.random.fold_in(streams_of[6], 71), 0),
        "page_slot": draw_page_slot(jax.random.fold_in(streams_of[6], 71), 0),
        "cached_len": draw_cached_len(jax.random.fold_in(streams_of[6], 71), 0),
    }


def reference(queries, new_kv, pool, page_owner, page_slot, cached_len):
    group_size = QH // KVH
    score_scale = 1.0 / math.sqrt(HD)
    positions = jnp.arange(CTX + NEW, dtype=jnp.int32)
    tokens_now = jnp.arange(NEW, dtype=jnp.int32)

    def one_request(request_no):
        query_rows = queries[request_no].reshape(NEW, KVH, group_size, HD)
        page_ids = (page_owner[request_no] * PAGES_DEV + page_slot[request_no]).astype(jnp.int32)
        cached = jnp.take(pool, page_ids, axis=0).reshape(MAXPG * PAGE, KVH, 2, HD)
        fresh = new_kv[request_no].reshape(NEW, KVH, 2, HD)
        key_rows = jnp.concatenate([cached[:, :, 0], fresh[:, :, 0]], axis=0)
        value_rows = jnp.concatenate([cached[:, :, 1], fresh[:, :, 1]], axis=0)
        cached_seen = (positions < cached_len[request_no])[None, :]
        fresh_seen = (positions - CTX)[None, :] <= tokens_now[:, None]
        visible = jnp.where((positions < CTX)[None, :], cached_seen, fresh_seen)

        def one_head(head_no):
            head_query = query_rows[:, head_no].astype(jnp.float32)
            head_keys = key_rows[:, head_no].astype(jnp.float32)
            scores = jnp.einsum('igd,kd->gik', head_query, head_keys) * score_scale
            scores = jnp.where(visible[None], scores, -jnp.inf)
            row_peak = lax.optimization_barrier(jnp.max(scores, axis=-1, keepdims=True))
            numer = jnp.exp(scores - row_peak)
            row_total = lax.optimization_barrier(jnp.sum(numer, axis=-1))
            weights = numer.astype(jnp.bfloat16)
            result = jnp.einsum('gik,kd->gid', weights.astype(jnp.float32), value_rows[:, head_no].astype(jnp.float32))
            return result / row_total[..., None]
        heads_out = lax.map(one_head, jnp.arange(KVH, dtype=jnp.int32))
        return heads_out.transpose(2, 0, 1, 3).reshape(NEW, QH * HD).astype(jnp.bfloat16)
    return lax.map(one_request, jnp.arange(REQS, dtype=jnp.int32))
```

```python
import functools
import math

import jax
import jax.numpy as jnp
from jax import lax
from jax.experimental import pallas as pl
from jax.experimental.pallas import tpu as pltpu
from jax.sharding import PartitionSpec as P

HD = 128
MESH = pl.DeviceIdType.MESH


def partner_of(me, k):
    out = me
    bit = 1
    while bit <= k:
        if k & bit:
            out = out + bit * (1 - 2 * ((me // bit) % 2))
        bit *= 2
    return out


def collect_kernel(count, slot_ref, pool_ref, out_ref, sems):
    def start(i, carry):
        pltpu.make_async_copy(pool_ref.at[slot_ref[i]], out_ref.at[i], sems.at[i]).start()
        return carry

    def finish(i, carry):
        pltpu.make_async_copy(pool_ref.at[0], out_ref.at[i], sems.at[i]).wait()
        return carry

    lax.fori_loop(0, count, start, 0)
    lax.fori_loop(0, count, finish, 0)


def attend_kernel(
    n, cap, valid_ref, q_ref, fresh_ref, outgoing_ref, out_ref,
    recv, peak, total, acc, send_sems, recv_sems,
):
    me = lax.axis_index("pool")
    heads, new_tok, _ = q_ref.shape
    page_len = recv.shape[1] // cap
    kv_dev = fresh_ref.shape[1] // (2 * HD)
    group = heads // kv_dev
    scale2 = math.log2(math.e) / math.sqrt(HD)

    barrier = pltpu.get_barrier_semaphore()
    for k in range(1, n):
        pl.semaphore_signal(
            barrier, inc=1, device_id={"pool": partner_of(me, k)}, device_id_type=MESH
        )
    own_copy = pltpu.make_async_copy(outgoing_ref.at[0], recv.at[0], recv_sems.at[0])
    own_copy.start()
    pl.semaphore_wait(barrier, n - 1)
    sends = []
    for k in range(n - 1, 0, -1):
        send = pltpu.make_async_remote_copy(
            src_ref=outgoing_ref.at[k],
            dst_ref=recv.at[k],
            send_sem=send_sems.at[k],
            recv_sem=recv_sems.at[k],
            device_id={"pool": partner_of(me, k)},
            device_id_type=MESH,
        )
        send.start()
        sends.append(send)

    def scores_of(keys, h):
        return lax.dot_general(
            keys, q_ref[h], (((1,), (1,)), ((), ())), preferred_element_type=jnp.float32
        )

    def weigh(values, weights):
        return lax.dot_general(
            values, weights, (((0,), (0,)), ((), ())), preferred_element_type=jnp.float32
        )

    key_no = lax.broadcasted_iota(jnp.int32, (new_tok, new_tok), 0)
    tok_no = lax.broadcasted_iota(jnp.int32, (new_tok, new_tok), 1)
    for g in range(kv_dev):
        keys = fresh_ref[:, 2 * g * HD : (2 * g + 1) * HD]
        values = fresh_ref[:, (2 * g + 1) * HD : (2 * g + 2) * HD]

        def first(i, carry):
            h = g * group + i
            s = jnp.where(key_no <= tok_no, scores_of(keys, h), -jnp.inf)
            top = jnp.max(s, axis=0, keepdims=True)
            w = jnp.exp2((s - top) * scale2)
            peak[h] = top
            total[h] = jnp.sum(w, axis=0, keepdims=True)
            acc[h] = weigh(values, w.astype(jnp.bfloat16))
            return carry

        lax.fori_loop(0, group, first, 0)

    rows = lax.broadcasted_iota(jnp.int32, (page_len, new_tok), 0)

    def attend(k):
        limits = [valid_ref[k * cap + j] for j in range(cap)]
        for g in range(kv_dev):

            def one_head(h):
                keys = recv[k, :, 2 * g * HD : (2 * g + 1) * HD]
                values = recv[k, :, (2 * g + 1) * HD : (2 * g + 2) * HD]
                s = scores_of(keys, h)
                s = jnp.concatenate(
                    [
                        jnp.where(
                            rows < limits[j], s[j * page_len : (j + 1) * page_len], -jnp.inf
                        )
                        for j in range(cap)
                    ],
                    axis=0,
                )
                before = peak[h]
                top = jnp.maximum(before, jnp.max(s, axis=0, keepdims=True))
                w = jnp.exp2((s - top) * scale2)
                factor = jnp.exp2((before - top) * scale2)
                peak[h] = top
                total[h] = total[h] * factor + jnp.sum(w, axis=0, keepdims=True)
                acc[h] = acc[h] * factor + weigh(values, w.astype(jnp.bfloat16))

            def two_heads(i, carry):
                one_head(g * group + 2 * i)
                one_head(g * group + 2 * i + 1)
                return carry

            lax.fori_loop(0, group // 2, two_heads, 0)

    own_copy.wait()
    attend(0)

    def one_block(k, carry):
        pltpu.make_async_copy(recv.at[k], recv.at[k], recv_sems.at[k]).wait()
        attend(k)
        return carry

    lax.fori_loop(1, n, one_block, 0)
    for h in range(heads):
        out_ref[:, h * HD : (h + 1) * HD] = (acc[h] / total[h]).T.astype(out_ref.dtype)
    for send in sends:
        send.wait_send()


def on_device(queries, new_kv, pool, page_owner, page_slot, cached_len):
    n = lax.axis_size("pool")
    me = lax.axis_index("pool")
    page_len, width = pool.shape[1], pool.shape[2]
    max_pages = page_owner.shape[1]
    cap = max_pages // n
    new_tok = queries.shape[1]
    heads = queries.shape[2] // HD
    page_no = jnp.arange(max_pages, dtype=jnp.int32)
    places = jnp.arange(cap, dtype=jnp.int32)
    partners = jnp.bitwise_xor(me, jnp.arange(n, dtype=jnp.int32))

    same = (page_owner[:, :, None] == page_owner[:, None, :]) & (
        page_no[None, None, :] < page_no[None, :, None]
    )
    rank = jnp.sum(same.astype(jnp.int32), axis=2)
    mine = (page_owner == me)[:, None, :] & (rank[:, None, :] == places[None, :, None])
    slots = jnp.sum(jnp.where(mine, page_slot[:, None, :], 0), axis=2)
    pick = (partners[:, None] == jnp.arange(n, dtype=jnp.int32)[None, :]).astype(jnp.int32)
    slots = jnp.sum(pick[:, :, None] * slots[None, :, :], axis=1).reshape(-1)

    is_me = jnp.arange(n, dtype=jnp.int32) == me
    my_owner = jnp.sum(jnp.where(is_me[:, None], page_owner, 0), axis=0)
    my_rank = jnp.sum(jnp.where(is_me[:, None], rank, 0), axis=0)
    my_len = jnp.sum(jnp.where(is_me, cached_len, 0))
    seen = jnp.clip(my_len - page_no * page_len, 0, page_len)
    hit = (my_owner[None, None, :] == partners[:, None, None]) & (
        my_rank[None, None, :] == places[None, :, None]
    )
    valid = jnp.sum(jnp.where(hit, seen[None, None, :], 0), axis=2).reshape(-1)

    outgoing = pl.pallas_call(
        functools.partial(collect_kernel, n * cap),
        out_shape=jax.ShapeDtypeStruct((n * cap, page_len, width), pool.dtype),
        in_specs=[pl.BlockSpec(memory_space=pltpu.SMEM), pl.BlockSpec(memory_space=pl.ANY)],
        out_specs=pl.BlockSpec(memory_space=pl.ANY),
        scratch_shapes=[pltpu.SemaphoreType.DMA((n * cap,))],
        name="collect",
    )(slots, pool)
    outgoing = outgoing.reshape(n, cap * page_len, width)

    q_heads = queries[0].reshape(new_tok, heads, HD).transpose(1, 0, 2)
    vmem = pl.BlockSpec(memory_space=pltpu.VMEM)
    out = pl.pallas_call(
        functools.partial(attend_kernel, n, cap),
        out_shape=jax.ShapeDtypeStruct((new_tok, heads * HD), jnp.bfloat16),
        in_specs=[
            pl.BlockSpec(memory_space=pltpu.SMEM), vmem, vmem, pl.BlockSpec(memory_space=pl.ANY)
        ],
        out_specs=vmem,
        scratch_shapes=[
            pltpu.VMEM((n, cap * page_len, width), jnp.bfloat16),
            pltpu.VMEM((heads, 1, new_tok), jnp.float32),
            pltpu.VMEM((heads, 1, new_tok), jnp.float32),
            pltpu.VMEM((heads, HD, new_tok), jnp.float32),
            pltpu.SemaphoreType.DMA((n,)),
            pltpu.SemaphoreType.DMA((n,)),
        ],
        compiler_params=pltpu.CompilerParams(
            collective_id=0, has_side_effects=True, vmem_limit_bytes=48 * 1024 * 1024
        ),
        name="attend",
    )(valid, q_heads, new_kv[0], outgoing)
    return out[None]


def solution(mesh):
    split = P("pool", None, "head")
    return jax.shard_map(
        on_device,
        mesh=mesh,
        in_specs=(split, split, split, P(), P(), P()),
        out_specs=split,
        check_vma=False,
    )
```

```python
import functools
import math

import jax
import jax.numpy as jnp
from jax import lax
from jax.experimental import pallas as pl
from jax.experimental.pallas import tpu as pltpu
from jax.sharding import PartitionSpec as P

HD = 128
MESH = pl.DeviceIdType.MESH


def partner_of(me, k, n):
    out = me
    bit = 1
    while bit < n:
        out = out + bit * ((k // bit) % 2) * (1 - 2 * ((me // bit) % 2))
        bit *= 2
    return out


def collect_kernel(slot_ref, *refs):
    out_ref = refs[-1]
    for j, page_ref in enumerate(refs[:-1]):
        out_ref[j] = page_ref[0]


def page_spec(step, j, page_len, width):
    return pl.BlockSpec((1, page_len, width), lambda i, slot_ref: (slot_ref[i * step + j], 0, 0))


def attend_kernel(
    n, cap, valid_ref, q_ref, fresh_ref, outgoing_ref, out_ref,
    recv, turned, peak, total, acc, send_sems, recv_sems,
):
    me = lax.axis_index("pool")
    heads, _, new_tok = q_ref.shape
    page_len = recv.shape[1] // cap
    kv_dev = fresh_ref.shape[1] // (2 * HD)
    group = heads // kv_dev
    scale2 = math.log2(math.e) / math.sqrt(HD)

    barrier = pltpu.get_barrier_semaphore()
    for k in range(1, n):
        pl.semaphore_signal(
            barrier, inc=1, device_id={"pool": partner_of(me, k, n)}, device_id_type=MESH
        )
    own_copy = pltpu.make_async_copy(outgoing_ref.at[0], recv.at[0], recv_sems.at[0])
    own_copy.start()
    pl.semaphore_wait(barrier, n - 1)

    def send_of(k):
        return pltpu.make_async_remote_copy(
            src_ref=outgoing_ref.at[k],
            dst_ref=recv.at[k],
            send_sem=send_sems.at[k],
            recv_sem=recv_sems.at[k],
            device_id={"pool": partner_of(me, k, n)},
            device_id_type=MESH,
        )

    half, late = n // 2, n // 4
    for k in [*range(half, n - late), *range(half - 1, 0, -1)]:
        send_of(k).start()

    def scores_of(keys, h):
        return lax.dot_general(
            keys, q_ref[h], (((1,), (0,)), ((), ())), preferred_element_type=jnp.float32
        )

    def weigh(values, weights):
        return lax.dot_general(
            values, weights, (((1,), (0,)), ((), ())), preferred_element_type=jnp.float32
        )

    key_no = lax.broadcasted_iota(jnp.int32, (new_tok, new_tok), 0)
    tok_no = lax.broadcasted_iota(jnp.int32, (new_tok, new_tok), 1)
    for g in range(kv_dev):
        keys = fresh_ref[:, 2 * g * HD : (2 * g + 1) * HD]
        values = fresh_ref[:, (2 * g + 1) * HD : (2 * g + 2) * HD].T

        def first(i, carry):
            h = g * group + i
            s = jnp.where(key_no <= tok_no, scores_of(keys, h), -jnp.inf)
            top = jnp.max(s, axis=0, keepdims=True)
            w = jnp.exp2((s - top) * scale2)
            peak[h] = top
            total[h] = jnp.sum(w, axis=0, keepdims=True)
            acc[h] = weigh(values, w.astype(jnp.bfloat16))
            return carry

        lax.fori_loop(0, group, first, 0)

    rows = lax.broadcasted_iota(jnp.int32, (page_len, new_tok), 0)

    def attend(k):
        limits = [valid_ref[k * cap + j] for j in range(cap)]
        for g in range(kv_dev):
            turned[...] = recv[k, :, (2 * g + 1) * HD : (2 * g + 2) * HD].T

            def one_head(h):
                keys = recv[k, :, 2 * g * HD : (2 * g + 1) * HD]
                values = turned[...]
                s = scores_of(keys, h)
                s = jnp.concatenate(
                    [
                        jnp.where(
                            rows < limits[j], s[j * page_len : (j + 1) * page_len], -jnp.inf
                        )
                        for j in range(cap)
                    ],
                    axis=0,
                )
                before = peak[h]
                top = jnp.maximum(before, jnp.max(s, axis=0, keepdims=True))
                w = jnp.exp2((s - top) * scale2)
                factor = jnp.exp2((before - top) * scale2)
                peak[h] = top
                total[h] = total[h] * factor + jnp.sum(w, axis=0, keepdims=True)
                acc[h] = acc[h] * factor + weigh(values, w.astype(jnp.bfloat16))

            def two_heads(i, carry):
                one_head(g * group + 2 * i)
                one_head(g * group + 2 * i + 1)
                return carry

            lax.fori_loop(0, group // 2, two_heads, 0)

    own_copy.wait()
    attend(0)

    def one_block(k, carry):
        pltpu.make_async_copy(recv.at[k], recv.at[k], recv_sems.at[k]).wait()

        @pl.when((k >= half) & (k < half + late))
        def _():
            send_of(k + late).start()

        attend(k)
        return carry

    lax.fori_loop(1, n, one_block, 0)
    for h in range(heads):
        out_ref[:, h * HD : (h + 1) * HD] = (acc[h] / total[h]).T.astype(out_ref.dtype)
    for k in range(1, n):
        send_of(k).wait_send()


def on_device(queries, new_kv, pool, page_owner, page_slot, cached_len):
    n = lax.axis_size("pool")
    me = lax.axis_index("pool")
    page_len, width = pool.shape[1], pool.shape[2]
    max_pages = page_owner.shape[1]
    cap = max_pages // n
    new_tok = queries.shape[1]
    heads = queries.shape[2] // HD
    page_no = jnp.arange(max_pages, dtype=jnp.int32)
    places = jnp.arange(cap, dtype=jnp.int32)
    partners = jnp.bitwise_xor(me, jnp.arange(n, dtype=jnp.int32))

    same = (page_owner[:, :, None] == page_owner[:, None, :]) & (
        page_no[None, None, :] < page_no[None, :, None]
    )
    rank = jnp.sum(same.astype(jnp.int32), axis=2)
    mine = (page_owner == me)[:, None, :] & (rank[:, None, :] == places[None, :, None])
    slots = jnp.sum(jnp.where(mine, page_slot[:, None, :], 0), axis=2)
    pick = (partners[:, None] == jnp.arange(n, dtype=jnp.int32)[None, :]).astype(jnp.int32)
    slots = jnp.sum(pick[:, :, None] * slots[None, :, :], axis=1).reshape(-1)

    is_me = jnp.arange(n, dtype=jnp.int32) == me
    my_owner = jnp.sum(jnp.where(is_me[:, None], page_owner, 0), axis=0)
    my_rank = jnp.sum(jnp.where(is_me[:, None], rank, 0), axis=0)
    my_len = jnp.sum(jnp.where(is_me, cached_len, 0))
    seen = jnp.clip(my_len - page_no * page_len, 0, page_len)
    hit = (my_owner[None, None, :] == partners[:, None, None]) & (
        my_rank[None, None, :] == places[None, :, None]
    )
    valid = jnp.sum(jnp.where(hit, seen[None, None, :], 0), axis=2).reshape(-1)

    step = math.gcd(n * cap, 4)
    outgoing = pl.pallas_call(
        collect_kernel,
        out_shape=jax.ShapeDtypeStruct((n * cap, page_len, width), pool.dtype),
        grid_spec=pltpu.PrefetchScalarGridSpec(
            num_scalar_prefetch=1,
            grid=(n * cap // step,),
            in_specs=[page_spec(step, j, page_len, width) for j in range(step)],
            out_specs=pl.BlockSpec((step, page_len, width), lambda i, slot_ref: (i, 0, 0)),
        ),
        compiler_params=pltpu.CompilerParams(vmem_limit_bytes=16 * 1024 * 1024),
        name="collect",
    )(slots, *([pool] * step))
    outgoing = outgoing.reshape(n, cap * page_len, width)

    q_heads = queries[0].reshape(new_tok, heads, HD).transpose(1, 2, 0)
    vmem = pl.BlockSpec(memory_space=pltpu.VMEM)
    out = pl.pallas_call(
        functools.partial(attend_kernel, n, cap),
        out_shape=jax.ShapeDtypeStruct((new_tok, heads * HD), jnp.bfloat16),
        in_specs=[
            pl.BlockSpec(memory_space=pltpu.SMEM), vmem, vmem, pl.BlockSpec(memory_space=pl.ANY)
        ],
        out_specs=vmem,
        scratch_shapes=[
            pltpu.VMEM((n, cap * page_len, width), jnp.bfloat16),
            pltpu.VMEM((HD, cap * page_len), jnp.bfloat16),
            pltpu.VMEM((heads, 1, new_tok), jnp.float32),
            pltpu.VMEM((heads, 1, new_tok), jnp.float32),
            pltpu.VMEM((heads, HD, new_tok), jnp.float32),
            pltpu.SemaphoreType.DMA((n,)),
            pltpu.SemaphoreType.DMA((n,)),
        ],
        compiler_params=pltpu.CompilerParams(
            collective_id=0, has_side_effects=True, vmem_limit_bytes=48 * 1024 * 1024
        ),
        name="attend",
    )(valid, q_heads, new_kv[0], outgoing)
    return out[None]


def solution(mesh):
    split = P("pool", None, "head")
    return jax.shard_map(
        on_device,
        mesh=mesh,
        in_specs=(split, split, split, P(), P(), P()),
        out_specs=split,
        check_vma=False,
    )
```
